32 devices in a mesh: segment: 2 (over x), space: 8 (over z, core), mirror: 2 (over y).
Axes of the slice: x: 2, y: 2, z: 4, core: 2. Of those that a mesh axis runs over, the one named last changes fastest.
Arguments:
- arrivals: bfloat16 [2, 2, 128, 128, 256], P('mirror', 'segment', 'space'), may hold values from -6 to 6
- stashed: bfloat16 [2, 2, 128, 128, 256], P('mirror', 'segment', 'space'), may hold values from -6 to 6
- weights: bfloat16 [2, 2, 2, 3, 3, 256, 256], P('mirror', 'segment'), may hold values from -0.125 to 0.125
Outputs:
- departures: bfloat16 [2, 2, 128, 128, 256], P('mirror', 'segment', 'space')
- grad_sum: float32 [2, 2, 256, 2, 3, 3, 256], P('mirror', 'segment', 'space')
The draws below stay inside these ranges and needn't reach their ends.
All inputs are finite; a program needn't handle non-finite values.
Results may differ from the reference program's by a relative error of at most 0.0053.
Values may be sent and summed in bfloat16 or wider, within the bound.
A program may use at most 128 MiB of HBM per device.

```python
import jax
import jax.numpy as jnp
from jax import lax

C = 256
CONVS = 2
COLS = 128
ROWS = 128
N_SEGMENT = 2
N_MIRROR = 2


def raised(values, rng, source, target, blocks, factor):
    owner, partner = [(jnp.arange(values.shape[position]) // (values.shape[position] // blocks)).reshape([-1 if axis == position else 1 for axis in range(values.ndim)]) for position in (source, target)]
    chosen = jax.random.permutation(rng, blocks)[partner]
    strong = (owner == chosen) | (owner == (partner + blocks // 2) % blocks)
    return jnp.where(strong, factor * values, values)


def shard_levels(key, shape, split, least, top_value):
    factor_of, own = 1.0, jax.random.fold_in(key, 6)
    for dim, parts in split:
        steps = jnp.exp(jax.random.uniform(jax.random.fold_in(own, dim), (parts,), jnp.float32, least / len(split), top_value / len(split)))
        factor_of = factor_of * jnp.repeat(steps, shape[dim] // parts).reshape([-1 if axis == dim else 1 for axis in range(len(shape))])
    return factor_of


def noise(key, extent, scale, limit, split=(), held_as=jnp.bfloat16):
    level = shard_levels(key, extent, split, -0.22, 0.18) if split else 1.0
    result = jax.random.normal(key, extent, jnp.float32) * scale * level
    return jnp.minimum(jnp.maximum(result, -limit), limit).astype(held_as)


def bell_draw_with(own_key, dims, spread, reach, pieces, heavy, kind=jnp.bfloat16):
    result = spread * jax.random.normal(own_key, dims, jnp.float32)
    if pieces:
        result = result * shard_levels(own_key, dims, pieces, -0.22, 0.18)
    return jnp.clip(raised(result, jax.random.fold_in(own_key, 3), *heavy), -reach, reach).astype(kind)


def setup_inputs(seed: int = 0) -> dict:
    seeds = jax.random.split(jax.random.key(seed), 4)
    return {
        "arrivals": noise(seeds[0], (N_MIRROR, N_SEGMENT, ROWS, COLS, C), 1.0, 6.0, ((0, 2), (1, 2), (2, 8))),
        "stashed": bell_draw_with(seeds[1], (N_MIRROR, N_SEGMENT, ROWS, COLS, C), 1.0, 6.0, ((0, 2), (1, 2), (2, 8)), (2, 4, 8, 2.0)),
        "weights": noise(seeds[2], (N_MIRROR, N_SEGMENT, CONVS, 3, 3, C, C), (9 * C) ** -0.5, 0.125, ((0, 2), (1, 2))),
    }


def convolve(padded, kernel):
    row_count = padded.shape[0] - 2
    col_count = padded.shape[1]
    widened = jnp.pad(padded, ((0, 0), (1, 1), (0, 0)))
    channels = kernel.shape[3]
    summed = jnp.zeros((row_count * col_count, channels), jnp.float32)
    for row_shift in range(3):
        for col_shift in range(3):
            window = widened[row_shift:row_shift + row_count, col_shift:col_shift + col_count].reshape(row_count * col_count, -1)
            summed = summed + jnp.dot(window, kernel[row_shift, col_shift], preferred_element_type=jnp.float32)
    return summed.reshape(row_count, col_count, channels)

def weight_grad(padded, cotangent):
    row_count = cotangent.shape[0]
    col_count = cotangent.shape[1]
    widened = jnp.pad(padded, ((0, 0), (1, 1), (0, 0)))
    flat_grad = cotangent.reshape(row_count * col_count, -1)
    entries = []
    for row_shift in range(3):
        row_list = []
        for col_shift in range(3):
            window = widened[row_shift:row_shift + row_count, col_shift:col_shift + col_count].reshape(row_count * col_count, -1)
            row_list.append(lax.dot_general(window, flat_grad, (((0,), (0,)), ((), ())), preferred_element_type=jnp.float32))
        entries.append(jnp.stack(row_list, axis=1))
    return jnp.stack(entries, axis=1)

def flipped(kernel):
    return jnp.transpose(kernel[::-1, ::-1], (0, 1, 3, 2))

def silu_slope(pre_act):
    sigmoid_val = jax.nn.sigmoid(pre_act)
    return sigmoid_val * (1.0 + pre_act * (1.0 - sigmoid_val))

def rows_padded(field_in):
    return jnp.pad(field_in, ((1, 1), (0, 0), (0, 0)))

def forward_section(field_in, kernels):
    pre_act = convolve(rows_padded(field_in), kernels[0])
    hidden = jax.nn.silu(pre_act).astype(jnp.bfloat16)
    return (field_in.astype(jnp.float32) + convolve(rows_padded(hidden), kernels[1])).astype(jnp.bfloat16)

def backward_section(field_in, cotangent, kernels, grad_scale):
    pre_act = convolve(rows_padded(field_in), kernels[0])
    hidden = jax.nn.silu(pre_act).astype(jnp.bfloat16)
    second = weight_grad(rows_padded(hidden), cotangent)
    inner_grad = (convolve(rows_padded(cotangent), flipped(kernels[1])) * silu_slope(pre_act)).astype(jnp.bfloat16)
    first = weight_grad(rows_padded(field_in), inner_grad)
    entering = (cotangent.astype(jnp.float32) + convolve(rows_padded(inner_grad), flipped(kernels[0]))).astype(jnp.bfloat16)
    return (entering, jnp.stack((first, second), axis=1) * grad_scale)

def reference(arrivals, stashed, weights):
    row_total = arrivals.shape[2]
    col_total = arrivals.shape[3]
    grad_scale = 1.0 / (row_total * col_total) ** 0.5
    leaving = [[None, None], [None, None]]
    grads = [[None, None], [None, None]]
    for replica in range(2):
        lead_pos = 0 if replica == 0 else 1
        tail_pos = 1 - lead_pos
        middle = forward_section(arrivals[replica, lead_pos], weights[replica, lead_pos])
        leaving[replica][tail_pos] = forward_section(middle, weights[replica, tail_pos])
        back_grad, grads[replica][tail_pos] = backward_section(stashed[replica, tail_pos], arrivals[replica, tail_pos], weights[replica, tail_pos], grad_scale)
        leaving[replica][lead_pos], grads[replica][lead_pos] = backward_section(stashed[replica, lead_pos], back_grad, weights[replica, lead_pos], grad_scale)
    departures = jnp.stack([jnp.stack(leaving[replica]) for replica in range(2)])
    totals = jnp.stack([jnp.stack([grads[replica][place] + grads[1 - replica][1 - place] for place in range(2)]) for replica in range(2)])
    return (departures, totals)
```

```python
import functools
import math

import jax
import jax.numpy as jnp
from jax import lax
from jax.experimental import pallas as pl
from jax.experimental.pallas import tpu as pltpu
from jax.sharding import PartitionSpec as P

F32 = jnp.float32
BF16 = jnp.bfloat16
MESH = pl.DeviceIdType.MESH


def divisor(total, most):
    return max(d for d in range(1, most + 1) if total % d == 0)


def kernel(
    sizes,
    arr,
    sta,
    wts,
    out,
    gout,
    a_buf,
    s_buf,
    r_buf,
    w3,
    wt3,
    x3,
    y3,
    slope,
    x_t,
    h_t,
    send_buf,
    gacc,
    gsend,
    pair_in,
    zsend,
    zrecv,
    owned,
    psend,
    precv,
    load_sem,
    halo_s,
    halo_r,
    swap_s,
    swap_r,
    pair_s,
    pair_r,
    z_s,
    z_r,
    part_s,
    part_r,
):
    rows, cols, ch, n, scale = sizes
    nz, share = n // 2, ch // n
    me = lax.axis_index("space")
    seg = lax.axis_index("segment")
    mir = lax.axis_index("mirror")
    parity, mine = lax.rem(me, 2), lax.div(me, 2)
    lead = seg == mir
    has_up, has_down = me > 0, me < n - 1
    out_rows = divisor(rows, 4)
    chunks = rows // out_rows
    pre_rows = divisor(rows + 2, 6)
    partner = {"segment": 1 - seg}
    twin = {"segment": 1 - seg, "mirror": 1 - mir}

    def span(first, count):
        return pl.ds(pl.multiple_of(first * cols, cols), count * cols)

    loads = [
        pltpu.make_async_copy(arr, a_buf.at[span(2, rows)], load_sem.at[0]),
        pltpu.make_async_copy(sta, s_buf.at[span(2, rows)], load_sem.at[1]),
        pltpu.make_async_copy(wts, w3, load_sem.at[2]),
    ]
    for load in loads:
        load.start()

    barrier = pltpu.get_barrier_semaphore()
    for k in range(1, n):
        pl.semaphore_signal(
            barrier, inc=1, device_id={"space": lax.rem(me + k, n)}, device_id_type=MESH
        )
    pl.semaphore_signal(barrier, inc=1, device_id=partner, device_id_type=MESH)
    pl.semaphore_signal(barrier, inc=1, device_id=twin, device_id_type=MESH)
    pl.semaphore_wait(barrier, n + 1)

    def up_copy(i, src, first, buf):
        return pltpu.make_async_remote_copy(
            src_ref=src.at[span(first, 2)],
            dst_ref=buf.at[span(rows + 2, 2)],
            send_sem=halo_s.at[i, 0],
            recv_sem=halo_r.at[i, 0],
            device_id={"space": me - 1},
            device_id_type=MESH,
        )

    def down_copy(i, src, first, buf):
        return pltpu.make_async_remote_copy(
            src_ref=src.at[span(first + rows - 2, 2)],
            dst_ref=buf.at[span(0, 2)],
            send_sem=halo_s.at[i, 1],
            recv_sem=halo_r.at[i, 1],
            device_id={"space": me + 1},
            device_id_type=MESH,
        )

    def halo_send_up(i, src, first, buf):
        @pl.when(has_up)
        def _():
            up_copy(i, src, first, buf).start()

    def halo_send_down(i, src, first, buf):
        @pl.when(has_down)
        def _():
            down_copy(i, src, first, buf).start()

    def halo_wait(i, src, first, buf):
        @pl.when(has_down)
        def _():
            up_copy(i, src, first, buf).wait_recv()

        @pl.when(has_up)
        def _():
            down_copy(i, src, first, buf).wait_recv()

        zeros = jnp.zeros((2 * cols, ch), BF16)

        @pl.when(jnp.logical_not(has_up))
        def _():
            buf[span(0, 2), :] = zeros

        @pl.when(jnp.logical_not(has_down))
        def _():
            buf[span(rows + 2, 2), :] = zeros

    def halo_drain(i, src, first, buf):
        @pl.when(has_up)
        def _():
            up_copy(i, src, first, buf).wait_send()

        @pl.when(has_down)
        def _():
            down_copy(i, src, first, buf).wait_send()

    halo_send_up(0, arr, 0, a_buf)
    halo_send_down(0, arr, 0, a_buf)
    halo_send_up(1, sta, 0, s_buf)
    halo_send_down(1, sta, 0, s_buf)

    loads[2].wait()

    @pl.loop(0, 2)
    def _(j):
        for a in range(3):
            for b in range(3):
                tile = w3[j, 2 - a, (2 - b) * ch : (3 - b) * ch, :]
                wt3[j, a, b * ch : (b + 1) * ch, :] = tile.T

    loads[0].wait()
    loads[1].wait()
    halo_wait(0, arr, 0, a_buf)
    halo_wait(1, sta, 0, s_buf)

    def widen(val, dst, first, count):
        shape = (count, cols, ch)
        col = lax.broadcasted_iota(jnp.int32, shape, 1)
        left = pltpu.roll(val, 1, 0).reshape(shape)
        right = pltpu.roll(val, count * cols - 1, 0).reshape(shape)
        flat = (count * cols, ch)
        dst[span(first, count), 0:ch] = (
            jnp.where(col == 0, 0.0, left).astype(BF16).reshape(flat)
        )
        dst[span(first, count), ch : 2 * ch] = val.astype(BF16)
        dst[span(first, count), 2 * ch : 3 * ch] = (
            jnp.where(col == cols - 1, 0.0, right).astype(BF16).reshape(flat)
        )

    def widen_all(src, dst):
        step = divisor(rows + 4, 4)

        @pl.loop(0, (rows + 4) // step)
        def _(k):
            widen(src[span(k * step, step), :].astype(F32), dst, k * step, step)

    def conv(src, kern, j, first, count):
        total = None
        for a in range(3):
            term = jnp.dot(
                src[span(first + a, count), :], kern[j, a], preferred_element_type=F32
            )
            total = term if total is None else total + term
        return total

    def clear_outside(dst):
        zeros = jnp.zeros((cols, 3 * ch), BF16)

        @pl.when(jnp.logical_not(has_up))
        def _():
            dst[span(0, 1), :] = zeros

        @pl.when(jnp.logical_not(has_down))
        def _():
            dst[span(rows + 1, 1), :] = zeros

    def transposed(dst, src, first, lanes):
        @pl.loop(0, chunks)
        def _(k):
            block = src[span(first + k * out_rows, out_rows), lanes]
            dst[:, span(k * out_rows, out_rows)] = block.T

    def hidden_forward(src3, dst3):
        @pl.loop(0, (rows + 2) // pre_rows)
        def _(k):
            pre = conv(src3, w3, 0, k * pre_rows, pre_rows)
            widen(pre * jax.nn.sigmoid(pre), dst3, k * pre_rows, pre_rows)

        clear_outside(dst3)

    def hidden_backward(src3, dst):
        @pl.loop(0, (rows + 2) // pre_rows)
        def _(k):
            pre = conv(src3, w3, 0, k * pre_rows, pre_rows)
            sig = jax.nn.sigmoid(pre)
            slope[span(k * pre_rows, pre_rows), :] = sig * (1.0 + pre * (1.0 - sig))
            dst[span(k * pre_rows, pre_rows), 0:ch] = (pre * sig).astype(BF16)

    def inner_backward(g3, dst3):
        @pl.loop(0, (rows + 2) // pre_rows)
        def _(k):
            val = conv(g3, wt3, 1, k * pre_rows, pre_rows)
            widen(val * slope[span(k * pre_rows, pre_rows), :], dst3, k * pre_rows, pre_rows)

        clear_outside(dst3)

    def swap_copy(k):
        return pltpu.make_async_remote_copy(
            src_ref=send_buf.at[span(k * out_rows, out_rows)],
            dst_ref=r_buf.at[span(2 + k * out_rows, out_rows)],
            send_sem=swap_s.at[k],
            recv_sem=swap_r.at[k],
            device_id=partner,
            device_id_type=MESH,
        )

    def finish_section(base, src3, kern, j, sending):
        @pl.loop(0, chunks)
        def _(step):
            k = lax.rem(chunks - step, chunks)
            val = base[span(2 + k * out_rows, out_rows), :].astype(F32)
            val = (val + conv(src3, kern, j, k * out_rows, out_rows)).astype(BF16)
            if sending:
                send_buf[span(k * out_rows, out_rows), :] = val
                swap_copy(k).start()
            else:
                out[span(k * out_rows, out_rows), :] = val

    def receive():
        swap_copy(0).wait_recv()
        if chunks > 1:
            swap_copy(chunks - 1).wait_recv()
        halo_send_up(2, r_buf, 2, r_buf)
        halo_send_down(2, r_buf, 2, r_buf)
        for k in range(1, chunks - 1):
            swap_copy(k).wait_recv()
        halo_wait(2, r_buf, 2, r_buf)

    def weight_grad(j, lhs_t, src3, first):
        @pl.loop(0, 3)
        def _(a):
            for b in range(3):
                val = scale * jnp.dot(
                    lhs_t[...],
                    src3[span(first + a, rows), b * ch : (b + 1) * ch],
                    preferred_element_type=F32,
                )
                lanes = pl.ds(pl.multiple_of(((2 - a) * 3 + (2 - b)) * ch, ch), ch)
                for owner in range(n):
                    gacc[j, owner % 2, owner // 2, :, lanes] = val[
                        owner * share : (owner + 1) * share
                    ]

    def pair_copy(j):
        return pltpu.make_async_remote_copy(
            src_ref=gsend.at[j],
            dst_ref=pair_in.at[j],
            send_sem=pair_s.at[j],
            recv_sem=pair_r.at[j],
            device_id={"space": me + 1 - 2 * parity},
            device_id_type=MESH,
        )

    def z_copy(j, k):
        return pltpu.make_async_remote_copy(
            src_ref=zsend.at[j, k],
            dst_ref=zrecv.at[j, k],
            send_sem=z_s.at[j, k],
            recv_sem=z_r.at[j, k],
            device_id={"space": 2 * lax.rem(mine + k + 1, nz) + parity},
            device_id_type=MESH,
        )

    def part_copy(j):
        return pltpu.make_async_remote_copy(
            src_ref=psend.at[j],
            dst_ref=precv.at[j],
            send_sem=part_s.at[j],
            recv_sem=part_r.at[j],
            device_id=twin,
            device_id_type=MESH,
        )

    def grads_to_pair(j):
        @pl.loop(0, nz)
        def _(z):
            gsend[j, z] = gacc[j, 1 - parity, z].astype(BF16)

        pair_copy(j).start()

    def grads_to_line(j):
        pair_copy(j).wait_recv()

        @pl.loop(0, nz - 1)
        def _(k):
            z = lax.rem(mine + k + 1, nz)
            zsend[j, k] = (gacc[j, parity, z] + pair_in[j, z].astype(F32)).astype(BF16)
            z_copy(j, k).start()

        owned[j] = gacc[j, parity, mine] + pair_in[j, mine].astype(F32)

    def grads_to_twin(j):
        total = owned[j]
        for k in range(nz - 1):
            z_copy(j, k).wait_recv()
            total = total + zrecv[j, k].astype(F32)
        owned[j] = total
        psend[j] = total.astype(BF16)
        part_copy(j).start()

    def grads_finish(j):
        part_copy(j).wait_recv()
        gout[j] = owned[j] + precv[j].astype(F32)

    mid = slice(0, ch)

    @pl.when(lead)
    def _():
        widen_all(a_buf, x3)
        hidden_forward(x3, y3)
        finish_section(a_buf, y3, w3, 1, True)
        widen_all(s_buf, x3)
        hidden_backward(x3, y3)
        transposed(h_t, y3, 1, mid)
        transposed(x_t, s_buf, 2, mid)
        receive()
        widen_all(r_buf, x3)
        weight_grad(1, h_t, x3, 1)
        grads_to_pair(1)
        inner_backward(x3, y3)
        grads_to_line(1)
        weight_grad(0, x_t, y3, 0)
        grads_to_pair(0)
        finish_section(r_buf, y3, wt3, 0, False)
        grads_to_line(0)

    @pl.when(jnp.logical_not(lead))
    def _():
        widen_all(s_buf, x3)
        hidden_backward(x3, y3)
        transposed(h_t, y3, 1, mid)
        widen_all(a_buf, x3)
        inner_backward(x3, y3)
        finish_section(a_buf, y3, wt3, 0, True)
        weight_grad(1, h_t, x3, 1)
        grads_to_pair(1)
        transposed(x_t, s_buf, 2, mid)
        weight_grad(0, x_t, y3, 0)
        grads_to_line(1)
        grads_to_pair(0)
        grads_to_line(0)
        receive()
        widen_all(r_buf, x3)
        hidden_forward(x3, y3)
        finish_section(r_buf, y3, w3, 1, False)

    grads_to_twin(1)
    grads_to_twin(0)
    grads_finish(1)
    grads_finish(0)

    halo_drain(0, arr, 0, a_buf)
    halo_drain(1, sta, 0, s_buf)
    halo_drain(2, r_buf, 2, r_buf)
    for k in range(chunks):
        swap_copy(k).wait_send()
    for j in range(2):
        pair_copy(j).wait_send()
        part_copy(j).wait_send()
        for k in range(nz - 1):
            z_copy(j, k).wait_send()


def body(arrivals, stashed, weights):
    _, _, rows, cols, ch = arrivals.shape
    n = lax.axis_size("space")
    nz, share = n // 2, ch // n
    scale = 1.0 / math.sqrt(rows * n * cols)
    out_chunks = rows // divisor(rows, 4)
    cells = rows * cols
    wide = 9 * ch
    dma = pltpu.SemaphoreType.DMA
    vm = pltpu.VMEM
    halo_cells = (rows + 4) * cols
    out, grads = pl.pallas_call(
        functools.partial(kernel, (rows, cols, ch, n, scale)),
        out_shape=(
            jax.ShapeDtypeStruct((cells, ch), BF16),
            jax.ShapeDtypeStruct((2, share, wide), F32),
        ),
        in_specs=[pl.BlockSpec(memory_space=pl.ANY)] * 3,
        out_specs=(pl.BlockSpec(memory_space=pltpu.VMEM),) * 2,
        scratch_shapes=[
            vm((halo_cells, ch), BF16),
            vm((halo_cells, ch), BF16),
            vm((halo_cells, ch), BF16),
            vm((2, 3, 3 * ch, ch), BF16),
            vm((2, 3, 3 * ch, ch), BF16),
            vm((halo_cells, 3 * ch), BF16),
            vm((halo_cells, 3 * ch), BF16),
            vm(((rows + 2) * cols, ch), F32),
            vm((ch, cells), BF16),
            vm((ch, cells), BF16),
            vm((cells, ch), BF16),
            vm((2, 2, nz, share, wide), F32),
            vm((2, nz, share, wide), BF16),
            vm((2, nz, share, wide), BF16),
            vm((2, nz - 1, share, wide), BF16),
            vm((2, nz - 1, share, wide), BF16),
            vm((2, share, wide), F32),
            vm((2, share, wide), BF16),
            vm((2, share, wide), BF16),
            dma((3,)),
            dma((3, 2)),
            dma((3, 2)),
            dma((out_chunks,)),
            dma((out_chunks,)),
            dma((2,)),
            dma((2,)),
            dma((2, nz - 1)),
            dma((2, nz - 1)),
            dma((2,)),
            dma((2,)),
        ],
        compiler_params=pltpu.CompilerParams(
            collective_id=0, has_side_effects=True, vmem_limit_bytes=56 * 1024 * 1024
        ),
    )(
        arrivals.reshape(cells, ch),
        stashed.reshape(cells, ch),
        weights.reshape(2, 3, 3 * ch, ch),
    )
    grads = jnp.transpose(grads.reshape(2, share, 3, 3, ch), (1, 0, 2, 3, 4))
    return (out.reshape(arrivals.shape), grads[None, None])


def solution(mesh):
    in_specs = (
        P("mirror", "segment", "space", None, None),
        P("mirror", "segment", "space", None, None),
        P("mirror", "segment", None, None, None, None, None),
    )
    out_specs = (
        P("mirror", "segment", "space", None, None),
        P("mirror", "segment", "space", None, None, None, None),
    )
    return jax.shard_map(body, mesh=mesh, in_specs=in_specs, out_specs=out_specs, check_vma=False)
```

```python
import functools
import math

import jax
import jax.numpy as jnp
from jax import lax
from jax.experimental import pallas as pl
from jax.experimental.pallas import tpu as pltpu
from jax.sharding import PartitionSpec as P

F32 = jnp.float32
BF16 = jnp.bfloat16
MESH = pl.DeviceIdType.MESH


def divisor(total, most):
    return max(d for d in range(1, most + 1) if total % d == 0)


def kernel(
    sizes,
    arr,
    sta,
    wts,
    out,
    gout,
    a_buf,
    s_buf,
    r_buf,
    w3,
    wt3,
    x3,
    y3,
    slope,
    h_buf,
    x_t,
    h_t,
    send_buf,
    gacc,
    gsend,
    pair_in,
    zsend,
    zrecv,
    owned,
    tsend,
    trecv,
    psend,
    precv,
    relay_in,
    load_sem,
    halo_s,
    halo_r,
    swap_s,
    swap_r,
    pair_s,
    pair_r,
    z_s,
    z_r,
    part_s,
    part_r,
    diag_s,
    diag_r,
    relay_s,
    relay_r,
    onward_s,
    onward_r,
):
    rows, cols, ch, n, scale = sizes
    nz, share = n // 2, ch // n
    me = lax.axis_index("space")
    seg = lax.axis_index("segment")
    mir = lax.axis_index("mirror")
    parity, mine = lax.rem(me, 2), lax.div(me, 2)
    lead = seg == mir
    has_up, has_down = me > 0, me < n - 1
    out_rows = divisor(rows, 4)
    chunks = rows // out_rows
    piece = out_rows // 2
    half = 9 * ch // 2
    my_lanes = pl.ds(pl.multiple_of(mir * half, half), half)
    twin_lanes = pl.ds(pl.multiple_of((1 - mir) * half, half), half)
    pre_rows = divisor(rows + 2, 6)
    partner = {"segment": 1 - seg}
    twin = {"segment": 1 - seg, "mirror": 1 - mir}
    relay = {"mirror": 1 - mir}

    def span(first, count):
        return pl.ds(pl.multiple_of(first * cols, cols), count * cols)

    loads = [
        pltpu.make_async_copy(arr, a_buf.at[span(2, rows)], load_sem.at[0]),
        pltpu.make_async_copy(sta, s_buf.at[span(2, rows)], load_sem.at[1]),
        pltpu.make_async_copy(wts, w3, load_sem.at[2]),
    ]
    for load in loads:
        load.start()

    barrier = pltpu.get_barrier_semaphore()
    for k in range(1, n):
        pl.semaphore_signal(
            barrier, inc=1, device_id={"space": lax.rem(me + k, n)}, device_id_type=MESH
        )
    pl.semaphore_signal(barrier, inc=1, device_id=partner, device_id_type=MESH)
    pl.semaphore_signal(barrier, inc=1, device_id=twin, device_id_type=MESH)
    pl.semaphore_signal(barrier, inc=1, device_id=relay, device_id_type=MESH)
    pl.semaphore_wait(barrier, n + 2)

    def up_copy(i, src, first, buf):
        return pltpu.make_async_remote_copy(
            src_ref=src.at[span(first, 2)],
            dst_ref=buf.at[span(rows + 2, 2)],
            send_sem=halo_s.at[i, 0],
            recv_sem=halo_r.at[i, 0],
            device_id={"space": me - 1},
            device_id_type=MESH,
        )

    def down_copy(i, src, first, buf):
        return pltpu.make_async_remote_copy(
            src_ref=src.at[span(first + rows - 2, 2)],
            dst_ref=buf.at[span(0, 2)],
            send_sem=halo_s.at[i, 1],
            recv_sem=halo_r.at[i, 1],
            device_id={"space": me + 1},
            device_id_type=MESH,
        )

    def halo_send_up(i, src, first, buf):
        @pl.when(has_up)
        def _():
            up_copy(i, src, first, buf).start()

    def halo_send_down(i, src, first, buf):
        @pl.when(has_down)
        def _():
            down_copy(i, src, first, buf).start()

    def halo_wait(i, src, first, buf):
        @pl.when(has_down)
        def _():
            up_copy(i, src, first, buf).wait_recv()

        @pl.when(has_up)
        def _():
            down_copy(i, src, first, buf).wait_recv()

        zeros = jnp.zeros((2 * cols, ch), BF16)

        @pl.when(jnp.logical_not(has_up))
        def _():
            buf[span(0, 2), :] = zeros

        @pl.when(jnp.logical_not(has_down))
        def _():
            buf[span(rows + 2, 2), :] = zeros

    def halo_drain(i, src, first, buf):
        @pl.when(has_up)
        def _():
            up_copy(i, src, first, buf).wait_send()

        @pl.when(has_down)
        def _():
            down_copy(i, src, first, buf).wait_send()

    halo_send_up(0, arr, 0, a_buf)
    halo_send_down(0, arr, 0, a_buf)
    halo_send_up(1, sta, 0, s_buf)
    halo_send_down(1, sta, 0, s_buf)

    loads[2].wait()

    def transpose_kernels():
        @pl.loop(0, 2)
        def _(j):
            for a in range(3):
                for b in range(3):
                    tile = w3[j, 2 - a, (2 - b) * ch : (3 - b) * ch, :]
                    wt3[j, a, b * ch : (b + 1) * ch, :] = tile.T

    @pl.when(jnp.logical_not(lead))
    def _():
        transpose_kernels()

    loads[0].wait()
    loads[1].wait()
    halo_wait(0, arr, 0, a_buf)
    halo_wait(1, sta, 0, s_buf)

    def widen(val, dst, first, count):
        shape = (count, cols, ch)
        col = lax.broadcasted_iota(jnp.int32, shape, 1)
        left = pltpu.roll(val, 1, 0).reshape(shape)
        right = pltpu.roll(val, count * cols - 1, 0).reshape(shape)
        flat = (count * cols, ch)
        dst[span(first, count), 0:ch] = (
            jnp.where(col == 0, 0.0, left).astype(BF16).reshape(flat)
        )
        dst[span(first, count), ch : 2 * ch] = val.astype(BF16)
        dst[span(first, count), 2 * ch : 3 * ch] = (
            jnp.where(col == cols - 1, 0.0, right).astype(BF16).reshape(flat)
        )

    def widen_all(src, dst):
        step = divisor(rows + 4, 4)

        @pl.loop(0, (rows + 4) // step)
        def _(k):
            widen(src[span(k * step, step), :].astype(F32), dst, k * step, step)

    def conv(src, kern, j, first, count):
        total = None
        for a in range(3):
            term = jnp.dot(
                src[span(first + a, count), :], kern[j, a], preferred_element_type=F32
            )
            total = term if total is None else total + term
        return total

    def clear_outside(dst):
        zeros = jnp.zeros((cols, 3 * ch), BF16)

        @pl.when(jnp.logical_not(has_up))
        def _():
            dst[span(0, 1), :] = zeros

        @pl.when(jnp.logical_not(has_down))
        def _():
            dst[span(rows + 1, 1), :] = zeros

    def transposed(dst, src, first, lanes):
        @pl.loop(0, chunks)
        def _(k):
            block = src[span(first + k * out_rows, out_rows), lanes]
            dst[:, span(k * out_rows, out_rows)] = block.T

    def hidden_forward(src3, dst3):
        @pl.loop(0, (rows + 2) // pre_rows)
        def _(k):
            pre = conv(src3, w3, 0, k * pre_rows, pre_rows)
            widen(pre * jax.nn.sigmoid(pre), dst3, k * pre_rows, pre_rows)

        clear_outside(dst3)

    def hidden_backward(src3, dst):
        @pl.loop(0, (rows + 2) // pre_rows)
        def _(k):
            pre = conv(src3, w3, 0, k * pre_rows, pre_rows)
            sig = jax.nn.sigmoid(pre)
            slope[span(k * pre_rows, pre_rows), :] = sig * (1.0 + pre * (1.0 - sig))
            dst[span(k * pre_rows, pre_rows), 0:ch] = (pre * sig).astype(BF16)

    def inner_backward(g3, dst3):
        @pl.loop(0, (rows + 2) // pre_rows)
        def _(k):
            val = conv(g3, wt3, 1, k * pre_rows, pre_rows)
            widen(val * slope[span(k * pre_rows, pre_rows), :], dst3, k * pre_rows, pre_rows)

        clear_outside(dst3)

    def swap_copy(q):
        return pltpu.make_async_remote_copy(
            src_ref=send_buf.at[span(q * piece, piece)],
            dst_ref=r_buf.at[span(2 + q * piece, piece)],
            send_sem=swap_s.at[q],
            recv_sem=swap_r.at[q],
            device_id=partner,
            device_id_type=MESH,
        )

    def relay_copy(k):
        return pltpu.make_async_remote_copy(
            src_ref=send_buf.at[span((2 * k + 1) * piece, piece)],
            dst_ref=relay_in.at[k],
            send_sem=relay_s.at[k],
            recv_sem=relay_r.at[k],
            device_id=relay,
            device_id_type=MESH,
        )

    def onward_copy(k):
        return pltpu.make_async_remote_copy(
            src_ref=relay_in.at[k],
            dst_ref=r_buf.at[span(2 + (2 * k + 1) * piece, piece)],
            send_sem=onward_s.at[k],
            recv_sem=onward_r.at[k],
            device_id=twin,
            device_id_type=MESH,
        )

    relayed = [0] + list(range(chunks - 2, 0, -1))
    direct_late = [q for q in range(2, 2 * chunks - 2)]
    direct_back = [q for q in range(2 * chunks) if q % 2 == 0 or q == 2 * chunks - 1]

    def finish_section(base, src3, kern, j, role):
        @pl.loop(0, chunks)
        def _(step):
            k = lax.rem(chunks - step, chunks)
            val = base[span(2 + k * out_rows, out_rows), :].astype(F32)
            val = (val + conv(src3, kern, j, k * out_rows, out_rows)).astype(BF16)
            if role is None:
                out[span(k * out_rows, out_rows), :] = val
                return
            send_buf[span(k * out_rows, out_rows), :] = val
            if role == "lead":

                @pl.when(step < 2)
                def _():
                    swap_copy(2 * k).start()
                    swap_copy(2 * k + 1).start()

            else:
                swap_copy(2 * k).start()

                @pl.when(k == chunks - 1)
                def _():
                    swap_copy(2 * k + 1).start()

                @pl.when(k < chunks - 1)
                def _():
                    relay_copy(k).start()

    def pass_on():
        for k in relayed:
            relay_copy(k).wait_recv()
            onward_copy(k).start()
        for q in direct_late:
            swap_copy(q).start()

    def receive(role):
        swap_copy(0).wait_recv()
        swap_copy(2 * chunks - 1).wait_recv()
        if piece < 2:
            swap_copy(2 * chunks - 2).wait_recv()
        halo_send_up(2, r_buf, 2, r_buf)
        halo_send_down(2, r_buf, 2, r_buf)
        skip = (0, 2 * chunks - 1) if piece >= 2 else (0, 2 * chunks - 1, 2 * chunks - 2)
        for q in direct_back if role == "lead" else range(2 * chunks):
            if q not in skip:
                swap_copy(q).wait_recv()
        if role == "lead":
            for k in relayed:
                onward_copy(k).wait_recv()
        halo_wait(2, r_buf, 2, r_buf)

    def weight_grad(j, lhs_t, src3, first):
        @pl.loop(0, 3)
        def _(a):
            for b in range(3):
                val = scale * jnp.dot(
                    lhs_t[...],
                    src3[span(first + a, rows), b * ch : (b + 1) * ch],
                    preferred_element_type=F32,
                )
                lanes = pl.ds(pl.multiple_of(((2 - a) * 3 + (2 - b)) * ch, ch), ch)
                for owner in range(n):
                    gacc[j, owner % 2, owner // 2, :, lanes] = val[
                        owner * share : (owner + 1) * share
                    ]

    def pair_copy(j):
        return pltpu.make_async_remote_copy(
            src_ref=gsend.at[j],
            dst_ref=pair_in.at[j],
            send_sem=pair_s.at[j],
            recv_sem=pair_r.at[j],
            device_id={"space": me + 1 - 2 * parity},
            device_id_type=MESH,
        )

    def z_copy(j, k):
        return pltpu.make_async_remote_copy(
            src_ref=zsend.at[j, k],
            dst_ref=zrecv.at[j, k],
            send_sem=z_s.at[j, k],
            recv_sem=z_r.at[j, k],
            device_id={"space": 2 * lax.rem(mine + k + 1, nz) + parity},
            device_id_type=MESH,
        )

    def part_copy(j):
        return pltpu.make_async_remote_copy(
            src_ref=psend.at[j],
            dst_ref=precv.at[j],
            send_sem=part_s.at[j],
            recv_sem=part_r.at[j],
            device_id=twin,
            device_id_type=MESH,
        )

    def grads_to_pair(j):
        @pl.loop(0, nz)
        def _(z):
            gsend[j, z] = gacc[j, 1 - parity, z].astype(BF16)

        pair_copy(j).start()

    def diag_copy(j):
        return pltpu.make_async_remote_copy(
            src_ref=tsend.at[j],
            dst_ref=trecv.at[j],
            send_sem=diag_s.at[j],
            recv_sem=diag_r.at[j],
            device_id=twin,
            device_id_type=MESH,
        )

    def grads_to_diag(j):
        pair_copy(j).wait_recv()

        @pl.loop(0, nz)
        def _(z):
            other = gacc[j, parity, z, :, twin_lanes]
            tsend[j, z] = (other + pair_in[j, z, :, twin_lanes].astype(F32)).astype(BF16)

        diag_copy(j).start()

    def summed(j, z):
        own = gacc[j, parity, z, :, my_lanes] + pair_in[j, z, :, my_lanes].astype(F32)
        return own + trecv[j, z].astype(F32)

    def grads_to_line(j):
        diag_copy(j).wait_recv()

        @pl.loop(0, nz - 1)
        def _(k):
            zsend[j, k] = summed(j, lax.rem(mine + k + 1, nz)).astype(BF16)
            z_copy(j, k).start()

        owned[j] = summed(j, mine)

    def grads_to_twin(j):
        total = owned[j]
        for k in range(nz - 1):
            z_copy(j, k).wait_recv()
            total = total + zrecv[j, k].astype(F32)
        gout[j, :, my_lanes] = total
        psend[j] = total.astype(BF16)
        part_copy(j).start()

    def grads_finish(j):
        part_copy(j).wait_recv()
        gout[j, :, twin_lanes] = precv[j].astype(F32)

    mid = slice(0, ch)

    @pl.when(lead)
    def _():
        widen_all(a_buf, x3)
        hidden_forward(x3, y3)
        finish_section(a_buf, y3, w3, 1, "lead")
        widen_all(s_buf, x3)
        hidden_backward(x3, h_buf)
        pass_on()
        transpose_kernels()
        transposed(h_t, h_buf, 1, mid)
        transposed(x_t, s_buf, 2, mid)
        receive("lead")
        widen_all(r_buf, x3)
        weight_grad(1, h_t, x3, 1)
        grads_to_pair(1)
        inner_backward(x3, y3)
        grads_to_diag(1)
        weight_grad(0, x_t, y3, 0)
        grads_to_pair(0)
        grads_to_line(1)
        grads_to_diag(0)
        finish_section(r_buf, y3, wt3, 0, None)
        grads_to_line(0)
        for q in range(2 * chunks):
            swap_copy(q).wait_send()
        for k in relayed:
            onward_copy(k).wait_send()

    @pl.when(jnp.logical_not(lead))
    def _():
        widen_all(s_buf, x3)
        hidden_backward(x3, h_buf)
        widen_all(a_buf, x3)
        inner_backward(x3, y3)
        finish_section(a_buf, y3, wt3, 0, "lag")
        transposed(h_t, h_buf, 1, mid)
        weight_grad(1, h_t, x3, 1)
        grads_to_pair(1)
        transposed(x_t, s_buf, 2, mid)
        weight_grad(0, x_t, y3, 0)
        grads_to_pair(0)
        for q in direct_back:
            swap_copy(q).wait_send()
        for k in relayed:
            relay_copy(k).wait_send()
        grads_to_diag(1)
        grads_to_diag(0)
        grads_to_line(1)
        grads_to_line(0)
        receive("lag")
        widen_all(r_buf, x3)
        hidden_forward(x3, y3)
        finish_section(r_buf, y3, w3, 1, None)

    grads_to_twin(1)
    grads_to_twin(0)
    grads_finish(1)
    grads_finish(0)

    halo_drain(0, arr, 0, a_buf)
    halo_drain(1, sta, 0, s_buf)
    halo_drain(2, r_buf, 2, r_buf)
    for j in range(2):
        pair_copy(j).wait_send()
        diag_copy(j).wait_send()
        part_copy(j).wait_send()
        for k in range(nz - 1):
            z_copy(j, k).wait_send()


def body(arrivals, stashed, weights):
    _, _, rows, cols, ch = arrivals.shape
    n = lax.axis_size("space")
    nz, share = n // 2, ch // n
    scale = 1.0 / math.sqrt(rows * n * cols)
    out_rows = divisor(rows, 4)
    out_chunks = rows // out_rows
    relays = max(out_chunks - 1, 1)
    half = 9 * ch // 2
    cells = rows * cols
    wide = 9 * ch
    dma = pltpu.SemaphoreType.DMA
    vm = pltpu.VMEM
    halo_cells = (rows + 4) * cols
    out, grads = pl.pallas_call(
        functools.partial(kernel, (rows, cols, ch, n, scale)),
        out_shape=(
            jax.ShapeDtypeStruct((cells, ch), BF16),
            jax.ShapeDtypeStruct((2, share, wide), F32),
        ),
        in_specs=[pl.BlockSpec(memory_space=pl.ANY)] * 3,
        out_specs=(pl.BlockSpec(memory_space=pltpu.VMEM),) * 2,
        scratch_shapes=[
            vm((halo_cells, ch), BF16),
            vm((halo_cells, ch), BF16),
            vm((halo_cells, ch), BF16),
            vm((2, 3, 3 * ch, ch), BF16),
            vm((2, 3, 3 * ch, ch), BF16),
            vm((halo_cells, 3 * ch), BF16),
            vm((halo_cells, 3 * ch), BF16),
            vm(((rows + 2) * cols, ch), F32),
            vm(((rows + 2) * cols, ch), BF16),
            vm((ch, cells), BF16),
            vm((ch, cells), BF16),
            vm((cells, ch), BF16),
            vm((2, 2, nz, share, wide), F32),
            vm((2, nz, share, wide), BF16),
            vm((2, nz, share, wide), BF16),
            vm((2, nz - 1, share, half), BF16),
            vm((2, nz - 1, share, half), BF16),
            vm((2, share, half), F32),
            vm((2, nz, share, half), BF16),
            vm((2, nz, share, half), BF16),
            vm((2, share, half), BF16),
            vm((2, share, half), BF16),
            vm((relays, out_rows // 2 * cols, ch), BF16),
            dma((3,)),
            dma((3, 2)),
            dma((3, 2)),
            dma((2 * out_chunks,)),
            dma((2 * out_chunks,)),
            dma((2,)),
            dma((2,)),
            dma((2, nz - 1)),
            dma((2, nz - 1)),
            dma((2,)),
            dma((2,)),
            dma((2,)),
            dma((2,)),
            dma((relays,)),
            dma((relays,)),
            dma((relays,)),
            dma((relays,)),
        ],
        compiler_params=pltpu.CompilerParams(
            collective_id=0, has_side_effects=True, vmem_limit_bytes=56 * 1024 * 1024
        ),
    )(
        arrivals.reshape(cells, ch),
        stashed.reshape(cells, ch),
        weights.reshape(2, 3, 3 * ch, ch),
    )
    grads = jnp.transpose(grads.reshape(2, share, 3, 3, ch), (1, 0, 2, 3, 4))
    return (out.reshape(arrivals.shape), grads[None, None])


def solution(mesh):
    in_specs = (
        P("mirror", "segment", "space", None, None),
        P("mirror", "segment", "space", None, None),
        P("mirror", "segment", None, None, None, None, None),
    )
    out_specs = (
        P("mirror", "segment", "space", None, None),
        P("mirror", "segment", "space", None, None, None, None),
    )
    return jax.shard_map(body, mesh=mesh, in_specs=in_specs, out_specs=out_specs, check_vma=False)
```
